32 devices in a mesh: geom: 2 (over y), gx: 4 (over z), gy: 2 (over x), gz: 2 (over core).
Axes of the slice: x: 2, y: 2, z: 4, core: 2. Of those that a mesh axis runs over, the one named last changes fastest.
Arguments:
- features: bfloat16 [20480, 128], P(('geom', 'gx', 'gy', 'gz')), parts along dimension 0, may hold values from -6 to 6
- displacement: float32 [3, 983040], P(None, ('geom', 'gx', 'gy', 'gz')), parts along dimension 1, as said below
- neighbour: int32 [983040], P(('geom', 'gx', 'gy', 'gz')), parts along dimension 0, may hold values from 0 to 2687, as said below
- neighbour_count: int32 [20480], P(('geom', 'gx', 'gy', 'gz')), parts along dimension 0, may hold values from 12 to 48, as said below
- species: int32 [20480], P(('geom', 'gx', 'gy', 'gz')), parts along dimension 0, may hold values from 0 to 99
- exports_x: int32 [32, 2, 640], P(('geom', 'gx', 'gy', 'gz')), parts along dimension 0, may hold values from 0 to 639, as said below
- exports_y: int32 [32, 2, 256], P(('geom', 'gx', 'gy', 'gz')), parts along dimension 0, may hold values from 0 to 639, as said below
- exports_z: int32 [32, 2, 128], P(('geom', 'gx', 'gy', 'gz')), parts along dimension 0, may hold values from 0 to 639, as said below
- face_counts: int32 [32, 6], P(('geom', 'gx', 'gy', 'gz')), parts along dimension 0, may hold values from 1 to 640, as said below
- w_in: bfloat16 [128, 128], replicated, may hold values from -0.5 to 0.5
- w_f1: bfloat16 [50, 128], replicated, may hold values from -1.75 to 1.75
- b_f1: float32 [128], replicated, may hold values from -3 to 3
- w_f2: bfloat16 [128, 128], replicated, may hold values from -0.125 to 0.125
- b_f2: float32 [128], replicated, may hold values from -3 to 3
- w_o1: bfloat16 [128, 128], replicated, may hold values from -0.5 to 0.5
- b_o1: float32 [128], replicated, may hold values from -3 to 3
- w_o2: bfloat16 [128, 128], replicated, may hold values from -0.5 to 0.5
- b_o2: float32 [128], replicated, may hold values from -3 to 3
- w_e1: bfloat16 [128, 64], replicated, may hold values from -0.5 to 0.5
- b_e1: float32 [64], replicated, may hold values from -3 to 3
- w_e2: float32 [64], replicated, may hold values from -1.5 to 1.5
- species_scale: float32 [100], replicated, may hold values from 0.5 to 4
- species_shift: float32 [100], replicated, may hold values from -1 to 1
Outputs:
- energy: float32 [20480], P(('geom', 'gx', 'gy', 'gz')), parts along dimension 0
- forces: float32 [3, 20480], P(None, ('geom', 'gx', 'gy', 'gz')), parts along dimension 1
The draws below stay inside these ranges and needn't reach their ends.
There are 2 independent parts, one for each index of `geom`. The reference program is written for one: setup_inputs(seed, part) draws one part's arguments, and reference() takes and returns one part's arrays. A program takes and returns all parts, laid end to end along the dimension named above; an argument that names none is the same for every part. Nothing has to cross between parts.
Inputs may be any that keep to these rules, and one draw needn't show every extreme that they name: `face_counts`: entry column f is the used length of that face's list: at most 640 for columns 0 and 1, 256 for 2 and 3, 128 for 4 and 5; in every column some domain uses its whole list. `exports_x`: each list row names distinct own atoms. `exports_y`: each list row names distinct own atoms. `exports_z`: each list row names distinct own atoms. `neighbour`: live slots name an own row or a ghost row below the used length of its block; slots beyond the live count hold arbitrary rows. `neighbour_count`: every domain has an atom with all 48 slots live. `displacement`: lengths lie between 0.9 and 4.9.
All inputs are finite; a program needn't handle non-finite values.
Results may differ from the reference program's by a relative error of at most 0.012.
Values may be sent and summed in bfloat16 or wider, within the bound.
A program may use at most 128 MiB of HBM per device.

```python
import math
import jax
import jax.numpy as jnp
import numpy as np
from jax import lax

F = 128
EHID = 64
NSPEC = 100
RBF = 50
NBR = 48
ATOM_DEV = 640
DOMAINS = 16
ATOMS = 10240
PAIRS = 491520
X_GHOSTS = 640
Y_GHOSTS = 256
Z_GHOSTS = 128
GHOSTS = 2048
N_GX = 4
N_GY = 2
N_GZ = 2


def face_caps():
    return jnp.array([X_GHOSTS, X_GHOSTS, Y_GHOSTS, Y_GHOSTS, Z_GHOSTS, Z_GHOSTS], jnp.int32)


def count_table(key):
    caps = face_caps()
    root = jax.random.fold_in(key, 101)
    raw_level = jax.random.randint(jax.random.fold_in(root, 1), (DOMAINS, 6), 0, 1 << 20)
    level = raw_level % caps[None, :] + 1
    squared = (level * level + caps[None, :] - 1) // caps[None, :]
    full_at = jax.random.randint(jax.random.fold_in(root, 2), (6,), 0, DOMAINS)
    domain_ids = jnp.arange(DOMAINS, dtype=jnp.int32)[:, None]
    return jnp.where(domain_ids == full_at[None, :], caps[None, :], squared).astype(jnp.int32)


def received_counts(key):
    table = count_table(key).reshape(N_GX, N_GY, N_GZ, 6)
    stacked = jnp.stack([jnp.roll(table[..., 1], 1, axis=0), jnp.roll(table[..., 0], -1, axis=0), jnp.roll(table[..., 3], 1, axis=1), jnp.roll(table[..., 2], -1, axis=1), jnp.roll(table[..., 5], 1, axis=2), jnp.roll(table[..., 4], -1, axis=2)], axis=-1)
    return stacked.reshape(DOMAINS, 6)


def live_counts(key):
    root = jax.random.fold_in(key, 303)
    counts = jax.random.randint(jax.random.fold_in(root, 1), (DOMAINS, ATOM_DEV), NBR // 4, NBR + 1)
    full_at = jax.random.randint(jax.random.fold_in(root, 2), (DOMAINS, 1), 0, ATOM_DEV)
    atom_ids = jnp.arange(ATOM_DEV, dtype=jnp.int32)[None, :]
    return jnp.where(atom_ids == full_at, NBR, counts).astype(jnp.int32)


def draw_face_counts(key, part):
    return count_table(key)


def draw_neighbour_count(key, part):
    return live_counts(key).reshape(-1)


def draw_neighbour(key, part):
    got_counts = received_counts(key)
    live = live_counts(key)
    offsets = jnp.array([0, X_GHOSTS, 2 * X_GHOSTS, 2 * X_GHOSTS + Y_GHOSTS, 2 * X_GHOSTS + 2 * Y_GHOSTS, 2 * X_GHOSTS + 2 * Y_GHOSTS + Z_GHOSTS], jnp.int32)
    root = jax.random.fold_in(key, 202)
    shape = (DOMAINS, ATOM_DEV, NBR)
    choose_ghost = jax.random.randint(jax.random.fold_in(root, 1), shape, 0, 10)
    block_id = jax.random.randint(jax.random.fold_in(root, 2), shape, 0, 6)
    raw_row = jax.random.randint(jax.random.fold_in(root, 3), shape, 0, 1 << 20)
    local_row = jax.random.randint(jax.random.fold_in(root, 4), shape, 0, ATOM_DEV)
    any_row = jax.random.randint(jax.random.fold_in(root, 5), shape, 0, ATOM_DEV + GHOSTS)
    block_count = jnp.take_along_axis(got_counts, block_id.reshape(DOMAINS, -1), axis=1).reshape(shape)
    ghost_row = ATOM_DEV + jnp.take(offsets, block_id) + raw_row % block_count
    live_row = jnp.where(choose_ghost < 4, ghost_row, local_row)
    slot_ids = jnp.arange(NBR, dtype=jnp.int32)[None, None, :]
    return jnp.where(slot_ids < live[:, :, None], live_row, any_row).astype(jnp.int32).reshape(-1)


def export_lists(key, salt, length):
    keys = jax.random.split(jax.random.fold_in(key, salt), DOMAINS * 2)
    orders = jax.vmap(lambda one_key: jax.random.permutation(one_key, ATOM_DEV))(keys)
    return orders[:, :length].reshape(DOMAINS, 2, length).astype(jnp.int32)


def draw_exports_x(key, part):
    return export_lists(key, 401, X_GHOSTS)


def draw_exports_y(key, part):
    return export_lists(key, 402, Y_GHOSTS)


def draw_exports_z(key, part):
    return export_lists(key, 403, Z_GHOSTS)


def draw_displacement(key, part):
    shape = (PAIRS,)
    radial_u = jax.random.uniform(jax.random.fold_in(key, 501), shape, jnp.float32)
    polar = jax.random.uniform(jax.random.fold_in(key, 502), shape, jnp.float32, -1.0, 1.0)
    azimuth = jax.random.uniform(jax.random.fold_in(key, 503), shape, jnp.float32, 0.0, 2.0 * math.pi)
    radius = 0.9 + 4.0 * radial_u
    side = jnp.sqrt(jnp.maximum(1.0 - polar * polar, 0.0))
    return jnp.stack([radius * side * jnp.cos(azimuth), radius * side * jnp.sin(azimuth), radius * polar]).astype(jnp.float32)


def draw_w_f1(key, part):
    root = jax.random.fold_in(key, 601)
    centres = jnp.arange(RBF, dtype=jnp.float32) * (5.0 / (RBF - 1))
    period = jax.random.uniform(jax.random.fold_in(root, 1), (F,), jnp.float32, 0.8, 2.0)
    phase = jax.random.uniform(jax.random.fold_in(root, 2), (F,), jnp.float32, 0.0, 2.0 * math.pi)
    sign_bit = jax.random.randint(jax.random.fold_in(root, 3), (F,), 0, 2)
    signs = 2.0 * sign_bit.astype(jnp.float32) - 1.0
    level_u = jax.random.uniform(jax.random.fold_in(root, 4), (F,), jnp.float32)
    amplitude = signs * (1.0 + 0.5 * level_u)
    noise = 0.2 * jax.random.normal(jax.random.fold_in(root, 5), (RBF, F), jnp.float32)
    wave = jnp.sin(2.0 * math.pi * centres[:, None] / period[None, :] + phase[None, :])
    values = amplitude[None, :] * wave + noise
    return jnp.clip(values, -1.75, 1.75).astype(jnp.bfloat16)


def set_ends(values, stream_key, least, largest):
    shape = values.shape
    place = [jax.random.randint(jax.random.fold_in(stream_key, axis), (), 0, shape[axis]) for axis in range(len(shape))]
    values = values.at[tuple(place)].set(least)
    longest = shape.index(max(shape))
    place[longest] = (place[longest] + 1) % shape[longest]
    return values.at[tuple(place)].set(largest)


def shard_levels(rng, shape, shards, least, high):
    def one(dim, blocks):
        steps = jax.random.uniform(jax.random.fold_in(jax.random.fold_in(rng, 6), dim), (blocks,), jnp.float32, least / len(shards), high / len(shards))
        return jnp.repeat(jnp.exp(steps), shape[dim] // blocks).reshape((-1,) + (1,) * (len(shape) - dim - 1))

    factor_of = one(*shards[0])
    for cut in shards[1:]:
        factor_of = factor_of * one(*cut)
    return factor_of


def cumulative_ranks(amount, slope):
    portions = [(1 << 20) // math.isqrt(rank ** slope) + 1 for rank in range(1, amount + 1)]
    scale = 1 + sum(portions) // (1 << 30)
    return np.cumsum(np.array([max(1, weight // scale) for weight in portions]))


def ranked(stream_key, extent, amount, slope):
    table = cumulative_ranks(amount, slope)
    ticket = jax.random.randint(jax.random.fold_in(stream_key, 1), extent, 0, int(table[amount - 1]))
    rank = jnp.searchsorted(jnp.asarray(table, jnp.int32), ticket, side="right")
    return jax.random.permutation(jax.random.fold_in(stream_key, 2), amount)[rank].astype(jnp.int32)


def scatter_about(stream_key, extent, scale, most, cuts=(), kind=jnp.bfloat16):
    entries = jax.random.normal(stream_key, extent, jnp.float32) * scale
    if len(cuts) > 0:
        entries = shard_levels(stream_key, extent, cuts, -0.22, 0.18) * entries
    return jnp.clip(entries, min=-most, max=most).astype(kind)


def setup_inputs(seed: int = 0, part: int = 0) -> dict:
    seeds = jax.random.split(jax.random.key(seed), 24)
    own_keys = jax.random.split(jax.random.fold_in(seeds[23], part), 24)
    return {
        "features": scatter_about(own_keys[0], (ATOMS, F), 1.0, 6.0, ((0, 16),)),
        "displacement": draw_displacement(jax.random.fold_in(jax.random.fold_in(seeds[23], part), 71), part),
        "neighbour": draw_neighbour(jax.random.fold_in(jax.random.fold_in(seeds[23], part), 71), part),
        "neighbour_count": draw_neighbour_count(jax.random.fold_in(jax.random.fold_in(seeds[23], part), 71), part),
        "species": set_ends(ranked(own_keys[4], (ATOMS,), NSPEC, 2), jax.random.fold_in(own_keys[4], 3), 0, NSPEC - 1).astype(jnp.int32),
        "exports_x": draw_exports_x(jax.random.fold_in(jax.random.fold_in(seeds[23], part), 71), part),
        "exports_y": draw_exports_y(jax.random.fold_in(jax.random.fold_in(seeds[23], part), 71), part),
        "exports_z": draw_exports_z(jax.random.fold_in(jax.random.fold_in(seeds[23], part), 71), part),
        "face_counts": draw_face_counts(jax.random.fold_in(jax.random.fold_in(seeds[23], part), 71), part),
        "w_in": scatter_about(seeds[9], (F, F), F ** -0.5, 0.5),
        "w_f1": draw_w_f1(jax.random.fold_in(seeds[23], 71), part),
        "b_f1": scatter_about(seeds[11], (F,), 1.0, 3.0, (), jnp.float32),
        "w_f2": scatter_about(seeds[12], (F, F), (16 * F) ** -0.5, 0.125),
        "b_f2": scatter_about(seeds[13], (F,), 0.5, 3.0, (), jnp.float32),
        "w_o1": scatter_about(seeds[14], (F, F), F ** -0.5, 0.5),
        "b_o1": scatter_about(seeds[15], (F,), 0.5, 3.0, (), jnp.float32),
        "w_o2": scatter_about(seeds[16], (F, F), F ** -0.5, 0.5),
        "b_o2": scatter_about(seeds[17], (F,), 0.5, 3.0, (), jnp.float32),
        "w_e1": scatter_about(seeds[18], (F, EHID), F ** -0.5, 0.5),
        "b_e1": scatter_about(seeds[19], (EHID,), 0.5, 3.0, (), jnp.float32),
        "w_e2": scatter_about(seeds[20], (EHID,), (EHID // 4) ** -0.5, 1.5, (), jnp.float32),
        "species_scale": jnp.clip(jnp.exp(jax.random.uniform(seeds[21], (NSPEC,), jnp.float32, math.log(0.5), math.log(4.0))), 0.5, 4.0),
        "species_shift": jnp.clip(jax.random.uniform(seeds[22], (NSPEC,), jnp.float32, -1.0, 1.0), -1.0, 1.0),
    }


GAMMA = 10.0
CUTOFF = 5.0
LOG_TWO = math.log(2.0)

def shifted_softplus(value):
    return jax.nn.softplus(value) - LOG_TWO

def block_terms(table, feat_rows, disp_rows, index_rows, count_rows, scale_rows, shift_rows, weights):
    w_f1, b_f1, w_f2, b_f2, w_o1, b_o1, w_o2, b_o2, w_e1, b_e1, w_e2 = weights
    row_count = feat_rows.shape[0]
    slot_count = index_rows.shape[0] // row_count
    width = feat_rows.shape[1]
    radial = w_f1.shape[0]
    distance = jnp.sqrt(lax.optimization_barrier(jnp.sum(disp_rows * disp_rows, axis=0)))
    centres = jnp.arange(radial, dtype=jnp.float32) * (CUTOFF / (radial - 1))
    offset = distance[None, :] - centres[:, None]
    basis_vals = jnp.exp(-GAMMA * offset * offset)
    basis_slope = -2.0 * GAMMA * offset * basis_vals
    phase_arg = jnp.pi * distance / CUTOFF
    envelope = 0.5 * (jnp.cos(phase_arg) + 1.0)
    envelope_slope = -0.5 * jnp.pi / CUTOFF * jnp.sin(phase_arg)
    slot_index = lax.broadcasted_iota(jnp.int32, (row_count, slot_count), 1)
    live_mask = (slot_index < count_rows[:, None]).astype(jnp.float32).reshape(-1)
    pre_act = lax.dot_general(basis_vals.astype(jnp.bfloat16), w_f1, (((0,), (0,)), ((), ())), preferred_element_type=jnp.float32) + b_f1
    hidden = shifted_softplus(pre_act).astype(jnp.bfloat16)
    filter_out = jnp.dot(hidden, w_f2, preferred_element_type=jnp.float32) + b_f2
    pair_weight = filter_out * (envelope * live_mask)[:, None]
    neighbour_rows = table[index_rows].astype(jnp.float32)
    message = lax.optimization_barrier(jnp.sum((neighbour_rows * pair_weight).reshape(row_count, slot_count, width), axis=1))
    out_pre = jnp.dot(message.astype(jnp.bfloat16), w_o1, preferred_element_type=jnp.float32) + b_o1
    out_mid = shifted_softplus(out_pre).astype(jnp.bfloat16)
    updated = feat_rows.astype(jnp.float32) + jnp.dot(out_mid, w_o2, preferred_element_type=jnp.float32) + b_o2
    energy_pre = jnp.dot(updated.astype(jnp.bfloat16), w_e1, preferred_element_type=jnp.float32) + b_e1
    energy = scale_rows * lax.optimization_barrier(jnp.sum(shifted_softplus(energy_pre) * w_e2[None, :], axis=1)) + shift_rows
    grad_head = (scale_rows[:, None] * w_e2[None, :] * jax.nn.sigmoid(energy_pre)).astype(jnp.bfloat16)
    grad_update = jnp.dot(grad_head, w_e1.T, preferred_element_type=jnp.float32).astype(jnp.bfloat16)
    grad_mid = (jnp.dot(grad_update, w_o2.T, preferred_element_type=jnp.float32) * jax.nn.sigmoid(out_pre)).astype(jnp.bfloat16)
    grad_message = jnp.dot(grad_mid, w_o1.T, preferred_element_type=jnp.float32)
    pair_grad = (grad_message[:, None, :] * neighbour_rows.reshape(row_count, slot_count, width)).reshape(-1, width) * live_mask[:, None]
    grad_filter = (pair_grad * envelope[:, None]).astype(jnp.bfloat16)
    grad_pre = (jnp.dot(grad_filter, w_f2.T, preferred_element_type=jnp.float32) * jax.nn.sigmoid(pre_act)).astype(jnp.bfloat16)
    grad_basis = lax.dot_general(w_f1, grad_pre, (((1,), (1,)), ((), ())), preferred_element_type=jnp.float32)
    grad_dist = lax.optimization_barrier(jnp.sum(grad_basis * basis_slope, axis=0)) + lax.optimization_barrier(jnp.sum(pair_grad * filter_out, axis=1)) * envelope_slope
    pair_force = disp_rows * (grad_dist / distance)[None, :]
    return (energy, pair_force)

def reference(features, displacement, neighbour, neighbour_count, species, exports_x, exports_y, exports_z, face_counts, w_in, w_f1, b_f1, w_f2, b_f2, w_o1, b_o1, w_o2, b_o2, w_e1, b_e1, w_e2, species_scale, species_shift):
    domains = N_GX * N_GY * N_GZ
    grid = (N_GX, N_GY, N_GZ)
    width = features.shape[1]
    x_local = jnp.dot(features, w_in, preferred_element_type=jnp.float32).astype(jnp.bfloat16).reshape(domains, ATOM_DEV, width)

    def export_rows(lists, column):
        picked = jax.vmap(lambda rows_all, index_row: rows_all[index_row])(x_local, lists)
        kept_mask = jnp.arange(lists.shape[1], dtype=jnp.int32)[None, :] < face_counts[:, column][:, None]
        picked = jnp.where(kept_mask[:, :, None], picked, jnp.zeros_like(picked))
        return picked.reshape(grid + picked.shape[1:])
    blocks_in = [jnp.roll(export_rows(exports_x[:, 1], 1), 1, axis=0), jnp.roll(export_rows(exports_x[:, 0], 0), -1, axis=0), jnp.roll(export_rows(exports_y[:, 1], 3), 1, axis=1), jnp.roll(export_rows(exports_y[:, 0], 2), -1, axis=1), jnp.roll(export_rows(exports_z[:, 1], 5), 1, axis=2), jnp.roll(export_rows(exports_z[:, 0], 4), -1, axis=2)]
    ghost_rows = jnp.concatenate([piece.reshape(domains, -1, width) for piece in blocks_in], axis=1)
    tables = jnp.concatenate([x_local, ghost_rows], axis=1)
    scale_all = species_scale[species]
    shift_all = species_shift[species]
    weights = (w_f1, b_f1, w_f2, b_f2, w_o1, b_o1, w_o2, b_o2, w_e1, b_e1, w_e2)

    def one_domain(pieces):
        table, feat_rows, disp_rows, index_rows, count_rows, scale_rows, shift_rows = pieces
        energy, pair_force = block_terms(table, feat_rows, disp_rows, index_rows, count_rows, scale_rows, shift_rows, weights)
        own_force = lax.optimization_barrier(jnp.sum(pair_force.reshape(3, ATOM_DEV, -1), axis=2))
        spread = jnp.zeros((3, table.shape[0]), jnp.float32).at[:, index_rows].add(-pair_force)
        return (energy, own_force + spread[:, :ATOM_DEV], spread[:, ATOM_DEV:])
    energy, forces, ghost_force = lax.map(one_domain, (tables, features.reshape(domains, ATOM_DEV, width), displacement.reshape(3, domains, -1).transpose(1, 0, 2), neighbour.reshape(domains, -1), neighbour_count.reshape(domains, -1), scale_all.reshape(domains, -1), shift_all.reshape(domains, -1)))
    ghost_force = ghost_force.reshape(grid + (3, -1))

    def return_block(forces, start, length, by, axis, lists, column):
        piece = jnp.roll(ghost_force[..., start:start + length], by, axis=axis).reshape(domains, 3, length)
        kept_mask = jnp.arange(length, dtype=jnp.int32)[None, :] < face_counts[:, column][:, None]
        piece = jnp.where(kept_mask[:, None, :], piece, jnp.zeros_like(piece))
        return jax.vmap(lambda total, index_row, values: total.at[:, index_row].add(values))(forces, lists, piece)
    start_y = 2 * X_GHOSTS
    start_z = 2 * X_GHOSTS + 2 * Y_GHOSTS
    forces = return_block(forces, 0, X_GHOSTS, -1, 0, exports_x[:, 1], 1)
    forces = return_block(forces, X_GHOSTS, X_GHOSTS, 1, 0, exports_x[:, 0], 0)
    forces = return_block(forces, start_y, Y_GHOSTS, -1, 1, exports_y[:, 1], 3)
    forces = return_block(forces, start_y + Y_GHOSTS, Y_GHOSTS, 1, 1, exports_y[:, 0], 2)
    forces = return_block(forces, start_z, Z_GHOSTS, -1, 2, exports_z[:, 1], 5)
    forces = return_block(forces, start_z + Z_GHOSTS, Z_GHOSTS, 1, 2, exports_z[:, 0], 4)
    return (energy.reshape(-1), forces.transpose(1, 0, 2).reshape(3, -1))
```

```python
import math

import jax
import jax.numpy as jnp
from jax import lax
from jax.experimental import pallas as pl
from jax.experimental.pallas import tpu as pltpu
from jax.sharding import PartitionSpec as P

GAMMA = 10.0
CUTOFF = 5.0
LOG_TWO = math.log(2.0)
LOG2E = 1.0 / LOG_TWO
LANES = 128
UNROLL = 4
PIECES = 4
CHUNK = 256
RADIAL_ROWS = 64
GROUP_ROWS = 24

BF16 = jnp.bfloat16
F32 = jnp.float32


def dot(a, b):
    return jnp.dot(a, b, preferred_element_type=F32)


def dot_nt(a, b):
    return lax.dot_general(a, b, (((1,), (1,)), ((), ())), preferred_element_type=F32)


def split3(value):
    high = value.astype(BF16)
    rest = value - high.astype(F32)
    middle = rest.astype(BF16)
    low = (rest - middle.astype(F32)).astype(BF16)
    return high, middle, low


def softplus_of(value):
    return jnp.maximum(value, 0.0) + jnp.log(1.0 + jnp.exp(-jnp.abs(value)))


def sigmoid_of(value):
    return 1.0 / (1.0 + jnp.exp(-value))


def flip(weight):
    return weight.astype(F32).T.astype(BF16)


def pair_kernel(
    disp_ref,
    index_ref,
    count_ref,
    species_ref,
    scale_ref,
    shift_ref,
    feat_ref,
    table_ref,
    w1_ref,
    b1_ref,
    w2_ref,
    wo1_ref,
    wo2_ref,
    we1_ref,
    bf2_ref,
    bo1_ref,
    bo2_ref,
    be1_ref,
    w_e2_ref,
    energy_ref,
    own_ref,
    spread_ref,
    dist_ref,
    env_ref,
    row_ref,
    s1_ref,
    s2_ref,
    msg_ref,
    gm_ref,
    xj_ref,
    prod_ref,
    sig_ref,
    slope_ref,
    pf_ref,
    piece_ref,
    total_ref,
):
    slots, atoms = index_ref.shape
    width = feat_ref.shape[1]
    piece_rows = piece_ref.shape[1]
    tiles = atoms // LANES
    steps = slots // UNROLL
    span = UNROLL * LANES
    radial = w1_ref.shape[0]

    table_rows = table_ref.shape[1]
    for q in range(PIECES):
        have = max(0, min(piece_rows, table_rows - q * piece_rows))
        band = slice(q * width, (q + 1) * width)
        if have:
            piece_ref[band, 0:have] = table_ref[:, q * piece_rows : q * piece_rows + have]
        if have < piece_rows:
            piece_ref[band, have:piece_rows] = jnp.zeros((width, piece_rows - have), BF16)

    atom_row = lax.broadcasted_iota(jnp.int32, (1, atoms), 1)
    atom_col = lax.broadcasted_iota(jnp.int32, (atoms, 1), 0)
    count_row = count_ref[...].reshape(1, atoms)
    key_row = (count_row * atoms - atom_row).astype(F32)
    count_col = jnp.broadcast_to(count_row.astype(F32), (128, atoms)).T[:, 0:1]
    key_col = count_col * float(atoms) - atom_col.astype(F32)
    rank_col = jnp.sum(jnp.where(key_row > key_col, 1.0, 0.0), axis=1, keepdims=True)
    perm = jnp.where(rank_col == atom_row.astype(F32), 1.0, 0.0).astype(BF16)

    def sort_exact(value):
        high, middle, low = split3(value)
        return dot(high, perm) + dot(middle, perm) + dot(low, perm)

    def unsort_exact(value):
        high, middle, low = split3(value)
        return dot_nt(high, perm) + dot_nt(middle, perm) + dot_nt(low, perm)

    def put(ref, value):
        for s in range(steps):
            ref[s] = value[s * UNROLL : (s + 1) * UNROLL]

    def take(ref):
        return jnp.concatenate([ref[s] for s in range(steps)], axis=0)

    disp = sort_exact(disp_ref[...])
    index = index_ref[...]
    index_high = dot((index >> 7).astype(F32).astype(BF16), perm)
    index_low = dot((index & 127).astype(F32).astype(BF16), perm)
    put(row_ref, index_high * 128.0 + index_low)
    counts = dot(
        jnp.broadcast_to(count_row, (8, atoms)).astype(F32).astype(BF16), perm
    )[0:1]
    kinds = scale_ref.shape[0]
    kind_ids = lax.broadcasted_iota(jnp.int32, (kinds, 1), 0)
    kind_pick = jnp.where(kind_ids == species_ref[...].reshape(1, atoms), 1.0, 0.0).astype(BF16)
    pair_of = jnp.concatenate(
        [
            jnp.broadcast_to(scale_ref[...].reshape(1, kinds), (8, kinds)),
            jnp.broadcast_to(shift_ref[...].reshape(1, kinds), (8, kinds)),
        ],
        axis=0,
    )
    atom_vals = sort_exact(sum(dot(part, kind_pick) for part in split3(pair_of)))
    scale = atom_vals[0:1]
    shift = atom_vals[8:9]
    feat = dot(feat_ref[...].astype(F32).T.astype(BF16), perm)

    dx = disp[0:slots]
    dy = disp[slots : 2 * slots]
    dz = disp[2 * slots : 3 * slots]
    squared = dx * dx + dy * dy + dz * dz
    distance = jnp.sqrt(squared)
    put(dist_ref, distance)
    slot_ids = lax.broadcasted_iota(jnp.int32, (slots, 1), 0).astype(F32)
    live = jnp.where(slot_ids < counts, 1.0, 0.0)
    y = (math.pi / CUTOFF) * distance - 0.5 * math.pi
    y2 = y * y
    sin_y = y * (
        1.0
        + y2
        * (
            -1.0 / 6
            + y2 * (1.0 / 120 + y2 * (-1.0 / 5040 + y2 * (1.0 / 362880 - y2 * (1.0 / 39916800))))
        )
    )
    envelope = (0.5 - 0.5 * sin_y) * live
    put(env_ref, envelope)
    s1_ref[...] = jnp.zeros_like(s1_ref)
    s2_ref[...] = jnp.zeros_like(s2_ref)

    bias = b1_ref[...].reshape(1, width)
    bias_high = bias.astype(BF16).astype(F32)
    bias_middle = (bias - bias_high).astype(BF16).astype(F32)
    w1 = jnp.concatenate(
        [
            w1_ref[...].astype(F32),
            bias_high,
            bias_middle,
            bias - bias_high - bias_middle,
            jnp.zeros((RADIAL_ROWS - radial - 3, width), F32),
        ],
        axis=0,
    )
    w1t = w1.T.astype(BF16)
    radial_col = lax.broadcasted_iota(jnp.int32, (RADIAL_ROWS, 1), 0)
    w1_back = jnp.where(radial_col < radial, w1, 0.0).astype(BF16)
    mu = radial_col.astype(F32) * (CUTOFF / (radial - 1))
    sharp = jnp.where(radial_col < radial, -GAMMA * LOG2E, 0.0)
    w2 = w2_ref[...]
    w2t = flip(w2)

    def column(ref):
        size = ref.shape[0]
        return jnp.broadcast_to(ref[...].reshape(1, size), (128, size)).T[:, 0:1]

    b_f2 = column(bf2_ref) * LOG2E
    b_o1 = column(bo1_ref)
    b_o2 = column(bo2_ref)
    b_e1 = column(be1_ref)
    w_e2 = column(w_e2_ref)

    def lane_row(ref, step, tile):
        return jnp.concatenate(
            [
                ref[step, u : u + 1, tile * LANES : (tile + 1) * LANES]
                for u in range(UNROLL)
            ],
            axis=1,
        )

    sizes = []
    left = piece_rows
    while left > 0:
        sizes.append(min(CHUNK, left))
        left -= sizes[-1]

    def gather(row):
        piece = jnp.zeros_like(row)
        for q in range(1, PIECES):
            piece = piece + jnp.where(row >= float(q * piece_rows), 1.0, 0.0)
        local = row - piece * float(piece_rows)
        parts = []
        start = 0
        for size in sizes:
            inside = (local >= float(start)) & (local < float(start + size))
            spot = jnp.where(inside, local - float(start), -1.0)
            spot = jnp.broadcast_to(spot, (16, span)).astype(BF16)
            lanes = lax.broadcasted_iota(jnp.int32, (16, span), 0).astype(F32)
            for b in range(size // 16):
                ids = (lanes + float(16 * b)).astype(BF16)
                parts.append(
                    jnp.where(ids == spot, jnp.ones((), BF16), jnp.zeros((), BF16))
                )
            start += size
        onehot = jnp.concatenate(parts, axis=0)
        found = dot(piece_ref[...], onehot)
        out = found[0:width]
        for q in range(1, PIECES):
            out = jnp.where(piece == float(q), found[q * width : (q + 1) * width], out)
        return out

    trips = []
    for tile in range(tiles):
        most = jnp.max(counts[:, tile * LANES : (tile + 1) * LANES]).astype(jnp.int32)
        trips.append((most + (UNROLL - 1)) // UNROLL)

    for tile in range(tiles):
        lanes = slice(tile * LANES, (tile + 1) * LANES)
        msg_ref[:, lanes] = jnp.zeros((width, LANES), F32)

        def forward(step, carry, tile=tile, lanes=lanes):
            at = tile * steps + step
            offset = lane_row(dist_ref, step, tile) - mu
            basis = jnp.exp2(sharp * (offset * offset))
            slope_ref[at] = (offset * basis).astype(BF16)
            pre = dot(w1t, basis.astype(BF16))
            grown = jnp.exp2(pre * LOG2E)
            total = 1.0 + grown
            sig_ref[at] = (grown * pl.reciprocal(total, approx=True)).astype(BF16)
            hidden = (jnp.log2(total) - 1.0).astype(BF16)
            filt = dot(w2t, hidden) + b_f2
            xj = gather(lane_row(row_ref, step, tile))
            xj_ref[at] = xj.astype(BF16)
            prod = xj * filt
            prod_ref[at] = prod.astype(BF16)
            weighted = prod * lane_row(env_ref, step, tile)
            part = msg_ref[:, lanes]
            for u in range(UNROLL):
                part = part + weighted[:, u * LANES : (u + 1) * LANES]
            msg_ref[:, lanes] = part
            return carry

        lax.fori_loop(0, trips[tile], forward, 0)

    wo1 = wo1_ref[...]
    wo2 = wo2_ref[...]
    we1 = we1_ref[...]
    message = (msg_ref[...] * LOG_TWO).astype(BF16)
    out_pre = dot(flip(wo1), message) + b_o1
    out_mid = (softplus_of(out_pre) - LOG_TWO).astype(BF16)
    updated = (feat + dot(flip(wo2), out_mid) + b_o2).astype(BF16)
    energy_pre = dot(we1, updated) + b_e1
    soft = softplus_of(energy_pre) - LOG_TWO
    energy = scale * jnp.sum(soft * w_e2, axis=0, keepdims=True) + shift
    grad_head = (scale * w_e2 * sigmoid_of(energy_pre)).astype(BF16)
    grad_update = dot(flip(we1), grad_head).astype(BF16)
    grad_mid = (dot(wo2, grad_update) * sigmoid_of(out_pre)).astype(BF16)
    gm_ref[...] = dot(wo1, grad_mid)

    for tile in range(tiles):
        lanes = slice(tile * LANES, (tile + 1) * LANES)

        def backward(step, carry, tile=tile, lanes=lanes):
            at = tile * steps + step
            grad = gm_ref[:, lanes]
            grad_wide = jnp.concatenate([grad] * UNROLL, axis=1)
            grad_b = grad.astype(BF16)
            grad_b_wide = jnp.concatenate([grad_b] * UNROLL, axis=1)
            mixed = dot(w2, grad_b_wide * xj_ref[at])
            grad_pre = (mixed * sig_ref[at].astype(F32)).astype(BF16)
            grad_basis = dot(w1_back, grad_pre)
            s1 = jnp.sum(grad_basis * slope_ref[at].astype(F32), axis=0, keepdims=True)
            s2 = jnp.sum(grad_wide * prod_ref[at].astype(F32), axis=0, keepdims=True)
            for u in range(UNROLL):
                piece = slice(u * LANES, (u + 1) * LANES)
                s1_ref[step, u : u + 1, lanes] = s1[:, piece]
                s2_ref[step, u : u + 1, lanes] = s2[:, piece]
            return carry

        lax.fori_loop(0, trips[tile], backward, 0)

    cos_y = 1.0 + y2 * (
        -0.5
        + y2
        * (
            1.0 / 24
            + y2
            * (
                -1.0 / 720
                + y2 * (1.0 / 40320 + y2 * (-1.0 / 3628800 + y2 * (1.0 / 479001600)))
            )
        )
    )
    env_slope = (-0.5 * math.pi / CUTOFF * LOG_TWO) * cos_y
    grad_dist = envelope * (-2.0 * GAMMA) * take(s1_ref) + env_slope * take(s2_ref)
    ratio = jnp.where(live > 0.5, grad_dist / distance, 0.0)
    fx = dx * ratio
    fy = dy * ratio
    fz = dz * ratio
    put(pf_ref.at[0], fx)
    put(pf_ref.at[1], fy)
    put(pf_ref.at[2], fz)
    own = jnp.concatenate(
        [jnp.sum(fx, axis=0, keepdims=True), jnp.sum(fy, axis=0, keepdims=True),
         jnp.sum(fz, axis=0, keepdims=True), energy, jnp.zeros((4, atoms), F32)],
        axis=0,
    )
    plain = unsort_exact(own)
    own_ref[...] = plain
    energy_ref[...] = plain[3:4].reshape(atoms)

    total_ref[...] = jnp.zeros_like(total_ref)
    spread_ref[...] = jnp.zeros_like(spread_ref)

    def spread(step, carry):
        group = lax.broadcasted_iota(jnp.int32, (GROUP_ROWS, 1), 0).astype(F32)
        low_ids = lax.broadcasted_iota(jnp.int32, (128, 1), 0).astype(F32)
        total = total_ref[...]
        for u in range(UNROLL):
            row = row_ref[step, u : u + 1, :]
            high = jnp.floor(row * (1.0 / 128))
            low = row - high * 128.0
            here = group == high
            placed = jnp.concatenate(
                [jnp.where(here, -pf_ref[c, step, u : u + 1, :], 0.0) for c in range(3)], axis=0
            ).astype(BF16)
            lower = jnp.where(low_ids == low, 1.0, 0.0).astype(BF16)
            total = total + dot_nt(placed, lower)
        total_ref[...] = total
        return carry

    lax.fori_loop(0, steps, spread, 0)
    for c in range(3):
        spread_ref[:, c, :] = total_ref[c * GROUP_ROWS : (c + 1) * GROUP_ROWS]


def neighbours():
    found = []
    for axis in ("gx", "gy", "gz"):
        size = lax.axis_size(axis)
        place = lax.axis_index(axis)
        found.append({axis: lax.rem(place + 1, size)})
        found.append({axis: lax.rem(place + size - 1, size)})
    return found


def greet(found):
    barrier = pltpu.get_barrier_semaphore()
    for device in found:
        pl.semaphore_signal(
            barrier, inc=1, device_id=device, device_id_type=pl.DeviceIdType.MESH
        )
    pl.semaphore_wait(barrier, len(found))


def picker(list_row, used, atoms):
    lanes = lax.broadcasted_iota(jnp.int32, list_row.shape, 1)
    names = jnp.where(lanes < used, list_row, -1).astype(F32)
    ids = lax.broadcasted_iota(jnp.int32, (atoms, 1), 0).astype(F32)
    return jnp.where(ids == names, 1.0, 0.0).astype(BF16)


FACES = ((0, 1, 1, 0), (0, 0, 0, 1), (1, 1, 3, 2), (1, 0, 2, 3), (2, 1, 5, 4), (2, 0, 4, 5))


def send_kernel(
    feat_ref, w_ref, ex_ref, ey_ref, ez_ref, used_ref, table_ref, stage_ref, send_sem, recv_sem
):
    atoms = feat_ref.shape[0]
    lists = (ex_ref, ey_ref, ez_ref)
    found = neighbours()
    x = dot(feat_ref[...], w_ref[...])
    x_t = x.T.astype(BF16)
    used = used_ref[...]
    greet(found)
    copies = []
    start = 0
    for n, (dim, side, column, to) in enumerate(FACES):
        length = lists[dim].shape[1]
        pick = picker(lists[dim][side : side + 1, :], used[:, column : column + 1], atoms)
        stage_ref[:, start : start + length] = dot(x_t, pick).astype(BF16)
        copy = pltpu.make_async_remote_copy(
            src_ref=stage_ref.at[:, pl.ds(start, length)],
            dst_ref=table_ref.at[:, pl.ds(atoms + start, length)],
            send_sem=send_sem.at[n],
            recv_sem=recv_sem.at[n],
            device_id=found[to],
            device_id_type=pl.DeviceIdType.MESH,
        )
        copy.start()
        copies.append(copy)
        start += length
    table_ref[:, 0:atoms] = x_t
    for copy in copies:
        copy.wait()


def return_kernel(
    own_ref,
    spread_ref,
    ex_ref,
    ey_ref,
    ez_ref,
    used_ref,
    force_ref,
    land_ref,
    send_sem,
    recv_sem,
):
    atoms = force_ref.shape[1]
    lists = (ex_ref, ey_ref, ez_ref)
    found = neighbours()
    greet(found)
    copies = []
    group = atoms // 128
    start = 0
    for n, (dim, side, column, to) in enumerate(FACES):
        length = lists[dim].shape[1] // 128
        copy = pltpu.make_async_remote_copy(
            src_ref=spread_ref.at[pl.ds(group + start, length)],
            dst_ref=land_ref.at[pl.ds(start, length)],
            send_sem=send_sem.at[n],
            recv_sem=recv_sem.at[n],
            device_id=found[to ^ 1],
            device_id_type=pl.DeviceIdType.MESH,
        )
        copy.start()
        copies.append(copy)
        start += length
    total = own_ref[...] + jnp.concatenate([spread_ref[h] for h in range(group)], axis=1)
    used = used_ref[...]
    start = 0
    for n, (dim, side, column, to) in enumerate(FACES):
        length = lists[dim].shape[1] // 128
        pick = picker(lists[dim][side : side + 1, :], used[:, column : column + 1], atoms)
        copies[n].wait()
        values = jnp.concatenate([land_ref[start + h] for h in range(length)], axis=1)
        high, middle, low = split3(values)
        total = total + dot_nt(high, pick) + dot_nt(middle, pick) + dot_nt(low, pick)
        start += length
    force_ref[...] = total[0:3]


def body(
    features,
    displacement,
    neighbour,
    neighbour_count,
    species,
    exports_x,
    exports_y,
    exports_z,
    face_counts,
    w_in,
    w_f1,
    b_f1,
    w_f2,
    b_f2,
    w_o1,
    b_o1,
    w_o2,
    b_o2,
    w_e1,
    b_e1,
    w_e2,
    species_scale,
    species_shift,
):
    atom_rows, width = features.shape
    slot_count = neighbour.shape[0] // atom_rows
    used_counts = face_counts[0]
    vmem = pl.BlockSpec(memory_space=pltpu.VMEM)
    lists = (exports_x[0], exports_y[0], exports_z[0])
    ghost_rows = sum(2 * one.shape[1] for one in lists)
    table_rows = atom_rows + ghost_rows
    table_t = pl.pallas_call(
        send_kernel,
        out_shape=jax.ShapeDtypeStruct((width, table_rows), BF16),
        in_specs=[vmem] * 6,
        out_specs=vmem,
        scratch_shapes=[
            pltpu.VMEM((width, ghost_rows), BF16),
            pltpu.SemaphoreType.DMA((6,)),
            pltpu.SemaphoreType.DMA((6,)),
        ],
        compiler_params=pltpu.CompilerParams(
            collective_id=0, has_side_effects=True, vmem_limit_bytes=32 * 1024 * 1024
        ),
    )(features, w_in, *lists, face_counts)
    piece_rows = -(-table_rows // (PIECES * CHUNK)) * CHUNK
    disp_t = (
        displacement.reshape(3, atom_rows, slot_count).transpose(0, 2, 1).reshape(-1, atom_rows)
    )
    index_t = neighbour.reshape(atom_rows, slot_count).T
    steps = slot_count // UNROLL * (atom_rows // LANES)
    span = UNROLL * LANES
    energy, own_force, spread = pl.pallas_call(
        pair_kernel,
        out_shape=(
            jax.ShapeDtypeStruct((atom_rows,), F32),
            jax.ShapeDtypeStruct((8, atom_rows), F32),
            jax.ShapeDtypeStruct((GROUP_ROWS, 8, 128), F32),
        ),
        in_specs=[vmem] * 19,
        out_specs=(vmem, vmem, vmem),
        scratch_shapes=[
            pltpu.VMEM((slot_count // UNROLL, UNROLL, atom_rows), F32),
            pltpu.VMEM((slot_count // UNROLL, UNROLL, atom_rows), F32),
            pltpu.VMEM((slot_count // UNROLL, UNROLL, atom_rows), F32),
            pltpu.VMEM((slot_count // UNROLL, UNROLL, atom_rows), F32),
            pltpu.VMEM((slot_count // UNROLL, UNROLL, atom_rows), F32),
            pltpu.VMEM((width, atom_rows), F32),
            pltpu.VMEM((width, atom_rows), F32),
            pltpu.VMEM((steps, width, span), BF16),
            pltpu.VMEM((steps, width, span), BF16),
            pltpu.VMEM((steps, width, span), BF16),
            pltpu.VMEM((steps, RADIAL_ROWS, span), BF16),
            pltpu.VMEM((3, slot_count // UNROLL, UNROLL, atom_rows), F32),
            pltpu.VMEM((PIECES * width, piece_rows), BF16),
            pltpu.VMEM((3 * GROUP_ROWS, 128), F32),
        ],
        compiler_params=pltpu.CompilerParams(vmem_limit_bytes=56 * 1024 * 1024),
        cost_estimate=pl.CostEstimate(
            flops=30_000_000_000, bytes_accessed=4_000_000, transcendentals=16_000_000
        ),
    )(
        disp_t,
        index_t,
        neighbour_count,
        species,
        species_scale,
        species_shift,
        features,
        table_t,
        w_f1,
        b_f1,
        w_f2,
        w_o1,
        w_o2,
        w_e1.T,
        b_f2,
        b_o1,
        b_o2,
        b_e1,
        w_e2,
    )
    forces = pl.pallas_call(
        return_kernel,
        out_shape=jax.ShapeDtypeStruct((3, atom_rows), F32),
        in_specs=[vmem] * 6,
        out_specs=vmem,
        scratch_shapes=[
            pltpu.VMEM((ghost_rows // 128, 8, 128), F32),
            pltpu.SemaphoreType.DMA((6,)),
            pltpu.SemaphoreType.DMA((6,)),
        ],
        compiler_params=pltpu.CompilerParams(
            collective_id=1, has_side_effects=True, vmem_limit_bytes=32 * 1024 * 1024
        ),
    )(own_force, spread, *lists, face_counts)
    return (energy, forces)


def solution(mesh):
    both = ("geom", "gx", "gy", "gz")
    return jax.shard_map(
        body,
        mesh=mesh,
        in_specs=(
            P(both, None),
            P(None, both),
            P(both),
            P(both),
            P(both),
            P(both, None, None),
            P(both, None, None),
            P(both, None, None),
            P(both, None),
        )
        + (P(),) * 14,
        out_specs=(P(both), P(None, both)),
        check_vma=False,
    )
```
